256 devices in a mesh: section: 4 (over x), col: 16 (over z_hi, y), dist: 4 (over z_lo, core).
Axes of the slice: x: 4, y: 4, z: 8 (z_hi: 4, z_lo: 2; z = z_hi * 2 + z_lo), core: 2. Of those that a mesh axis runs over, the one named last changes fastest.
Arguments:
- activations: bfloat16 [4, 1024, 14336], P('section', 'dist', 'col'), may hold values from -24 to 24
- out_grads: bfloat16 [4, 1024, 8192], P('section', 'dist', 'col'), may hold values from -24 to 24
- assign: int32 [9, 4], replicated, may hold values from 0 to 3, each once within a row
- act_old: bfloat16 [4, 9, 896, 14336], P('section', None, 'dist', 'col'), may hold values from -3 to 3
- grad_old: bfloat16 [4, 9, 512, 8192], P('section', None, 'dist', 'col'), may hold values from -3 to 3
Outputs:
- act_new: bfloat16 [4, 9, 896, 14336], P('section', None, 'dist', 'col')
- grad_new: bfloat16 [4, 9, 512, 8192], P('section', None, 'dist', 'col')
The draws below stay inside these ranges and needn't reach their ends.
Inputs may be any that keep to these rules, and one draw needn't show every extreme that they name: Each row of assign is a permutation of 0 to 4 - 1.
All inputs are finite; a program needn't handle non-finite values.
Results may differ from the reference program's by a relative error of at most 0.001.
Values may be sent and summed in bfloat16 or wider, within the bound.
A program may use at most 128 MiB of HBM per device.

```python
import math
import jax
import jax.numpy as jnp
from jax import lax

ACT_W = 14336
GRAD_W = 8192
SECTIONS = 4
TOKENS = 1024
DISTS = 9
ACT_PANEL = 896
GRAD_PANEL = 512
N_COL = 16
N_DIST = 4


def mixture(key, sections, rows, width, factor_weight, row_top, column_top):
    keys = jax.random.split(key, 6)
    normal = jax.random.normal(keys[0], (sections, rows, width), jnp.float32)
    values = normal
    loads = jax.random.normal(keys[2], (sections, rows, 4), jnp.float32)
    weights = jax.random.normal(keys[3], (sections, 4, width), jnp.float32) * factor_weight
    for factor in range(4):
        values = values + loads[:, :, factor:factor + 1] * weights[:, factor:factor + 1, :]
    row_scale = jnp.exp(jax.random.uniform(keys[4], (sections, rows, 1), jnp.float32, 0.0, math.log(row_top)))
    column_scale = jnp.exp(jax.random.uniform(keys[5], (sections, 1, width), jnp.float32, math.log(0.7), math.log(column_top)))
    return jnp.clip(values * row_scale * column_scale, -24.0, 24.0).astype(jnp.bfloat16)


def draw_activations(key, part):
    key = jax.random.fold_in(key, 11)
    return mixture(key, SECTIONS, TOKENS, ACT_W, 0.5, 1.0001, 1.4)


def draw_out_grads(key, part):
    key = jax.random.fold_in(key, 23)
    return mixture(key, SECTIONS, TOKENS, GRAD_W, 0.5, 1.0001, 1.4)


def steps_of(stream_key, dims, shards, least, top_value):
    factor_of = 1.0
    for position, blocks in shards:
        draws = jax.random.uniform(jax.random.fold_in(jax.random.fold_in(stream_key, 6), position), (blocks,), jnp.float32, least / len(shards), top_value / len(shards))
        factor_of = factor_of * jnp.repeat(jnp.exp(draws), dims[position] // blocks).reshape((-1,) + (1,) * (len(dims) - 1 - position))
    return factor_of


def normal_values(own_key, shape, scale, limit, cuts=(), kind=jnp.bfloat16):
    gain = steps_of(own_key, shape, cuts, -0.22, 0.18) if cuts else 1.0
    entries = jax.random.normal(own_key, shape, jnp.float32) * scale * gain
    return jnp.minimum(jnp.maximum(entries, -limit), limit).astype(kind)


def setup_inputs(seed: int = 0) -> dict:
    seeds = jax.random.split(jax.random.key(seed), 6)
    return {
        "activations": draw_activations(jax.random.fold_in(seeds[5], 71), 0),
        "out_grads": draw_out_grads(jax.random.fold_in(seeds[5], 71), 0),
        "assign": jax.vmap(lambda own: jax.random.permutation(own, N_DIST))(jax.random.split(seeds[2], DISTS)).reshape((DISTS, N_DIST)).astype(jnp.int32),
        "act_old": normal_values(seeds[3], (SECTIONS, DISTS, ACT_PANEL, ACT_W), 0.5, 3.0, ((0, 4), (2, 4), (3, 16))),
        "grad_old": normal_values(seeds[4], (SECTIONS, DISTS, GRAD_PANEL, GRAD_W), 0.5, 3.0, ((0, 4), (2, 4), (3, 16))),
    }


ema_decay = 0.75


def factor_blocks(rows, assign, panels, n_dist):
    tokens, width = rows.shape
    panel = width // panels
    strip = panel // n_dist
    grid = rows.astype(jnp.float32).reshape(tokens, panels, panel)

    def one_distance(inputs):
        distance, perm_row = inputs
        partner = jnp.roll(grid, -distance, axis=1)
        partner = partner.reshape(tokens, panels, n_dist, strip)
        partner = jnp.take(partner, perm_row, axis=2).reshape(tokens, panels, panel)
        product = jnp.einsum("tci,tcj->jci", grid, partner, precision=lax.Precision.HIGHEST)
        return product.reshape(panel, width) / tokens

    return lax.map(one_distance, (jnp.arange(assign.shape[0], dtype=jnp.int32), assign))


def blend(old_blocks, fresh):
    return (ema_decay * old_blocks.astype(jnp.float32) + (1.0 - ema_decay) * fresh).astype(jnp.bfloat16)


def reference(activations, out_grads, assign, act_old, grad_old):
    grads_in = jnp.roll(out_grads, -1, axis=0)

    def one_section(inputs):
        act_rows, grad_rows, old_act, old_grad = inputs
        act_fresh = factor_blocks(act_rows, assign, N_COL, N_DIST)
        grad_fresh = factor_blocks(grad_rows, assign, N_COL, N_DIST)
        return (blend(old_act, act_fresh), blend(old_grad, grad_fresh))

    act_new, grad_new = lax.map(one_section, (activations, grads_in, act_old, grad_old))
    return act_new, grad_new
```

```python
import functools
import jax
import jax.numpy as jnp
from jax import lax
from jax.experimental import pallas as pl
from jax.experimental.pallas import tpu as pltpu
from jax.sharding import PartitionSpec as P

ema_decay = 0.75
MESH = pl.DeviceIdType.MESH
NY = 4
NZ = 8
NX = 4


def kernel(
    act_ref, og_ref, assign_ref, olda_hbm, oldg_hbm, outa_hbm, outg_hbm,
    b0_a, p_a, c1_a, c2_a, c3_a, c4_a, oc0_a, ocp_a,
    b0_g, p_g, c1_g, c2_g, c3_g, c4_g, oc0_g, ocp_g,
    gbuf, stage_a, stage_g, recv_a, recv_g, olda, oldg,
    old_sem, out_sem, shift_sem, zsend, zrecv, ocsend, ocrecv, ysend, yrecv,
):
    x = lax.axis_index("section")
    c = lax.axis_index("col")
    q = lax.axis_index("dist")
    y, zh = lax.rem(c, NY), c // NY
    zl, k = q // 2, lax.rem(q, 2)
    z = 2 * zh + zl
    dists = olda.shape[0]
    parts = (
        dict(own=b0_a, p=p_a, c=(c1_a, c2_a, c3_a, c4_a), oc0=oc0_a, ocp=ocp_a,
             stage=stage_a, recv=recv_a, old=olda, out=outa_hbm, i=0),
        dict(own=b0_g, p=p_g, c=(c1_g, c2_g, c3_g, c4_g), oc0=oc0_g, ocp=ocp_g,
             stage=stage_g, recv=recv_g, old=oldg, out=outg_hbm, i=1),
    )

    def device(xx, zz, yy, kk):
        return (xx, (zz // 2) * NY + yy, lax.rem(zz, 2) * 2 + kk)

    z_down = device(x, lax.rem(z + NZ - 1, NZ), y, k)
    z_up = device(x, lax.rem(z + 1, NZ), y, k)
    twin = device(x, z, y, 1 - k)
    x_down = device(lax.rem(x + NX - 1, NX), z, y, k)
    x_up = device(lax.rem(x + 1, NX), z, y, k)

    old_copies = [
        pltpu.make_async_copy(olda_hbm, olda, old_sem.at[0]),
        pltpu.make_async_copy(oldg_hbm, oldg, old_sem.at[1]),
    ]

    barrier = pltpu.get_barrier_semaphore()
    greeted = [z_down, z_up, twin, x_down, x_up]
    for step in range(1, NY):
        for kk in range(2):
            greeted.append(device(x, z, lax.rem(y + step, NY), kk))
    for other in greeted:
        pl.semaphore_signal(barrier, inc=1, device_id=other, device_id_type=MESH)
    for copy in old_copies:
        copy.start()
    b0_a[...] = act_ref[...].T.reshape(b0_a.shape)
    pl.semaphore_wait(barrier, len(greeted))

    def remote(src, dst, send, recv, target):
        return pltpu.make_async_remote_copy(
            src_ref=src, dst_ref=dst, send_sem=send, recv_sem=recv,
            device_id=target, device_id_type=MESH,
        )

    shift = remote(og_ref, gbuf, shift_sem.at[0], shift_sem.at[1], x_down)
    shift.start()

    def z_copy(part, src, slot, dst, dst_slot, target):
        return remote(src, dst, zsend.at[part["i"], slot], zrecv.at[part["i"], dst_slot], target)

    def twin_copy(part, src, dst, slot):
        return remote(src, dst, ocsend.at[part["i"], slot], ocrecv.at[part["i"], slot], twin)

    def z_flows(part):
        cs = part["c"]
        return {
            "own": [
                (zl == 1, z_copy(part, part["own"], 0, part["p"], 0, z_down)),
                (zl == 0, z_copy(part, part["own"], 0, cs[0], 1, z_down)),
                (zl == 0, z_copy(part, part["own"], 6, part["p"], 0, z_up)),
            ],
            "p": [(zl == 0, z_copy(part, part["p"], 1, cs[1], 2, z_down))],
            "c0": [
                (zl == 0, z_copy(part, cs[0], 2, cs[2], 3, z_down)),
                (zl == 1, z_copy(part, cs[0], 2, cs[0], 1, z_down)),
            ],
            "c1": [
                (zl == 0, z_copy(part, cs[1], 3, cs[3], 4, z_down)),
                (zl == 1, z_copy(part, cs[1], 3, cs[1], 2, z_down)),
            ],
            "c2": [(zl == 1, z_copy(part, cs[2], 4, cs[2], 3, z_down))],
            "c3": [(zl == 1, z_copy(part, cs[3], 5, cs[3], 4, z_down))],
        }

    flows = [z_flows(part) for part in parts]

    def z_start(part, name):
        for condition, copy in flows[part["i"]][name]:
            pl.when(condition)(copy.start)

    def y_sends(part, source, dzh, zs):
        far = jnp.where(zs == zl, 0, 2)

        @pl.loop(0, NY)
        def _(yy):
            d = y + NY * dzh - yy

            @pl.when((d >= 1) & (d < dists))
            def _():
                for kk in range(2):
                    piece = part["stage"].at[d - 1, zs, kk]
                    piece[...] = source[assign_ref[d, 2 * zl + kk]]
                    here = (yy == y) & (k == kk)
                    place = part["recv"].at[d, far + jnp.where(k == kk, 0, 1)]
                    done = yrecv.at[part["i"], d]

                    @pl.when(here)
                    def _():
                        pltpu.make_async_copy(piece, place, done).start()

                    @pl.when(jnp.logical_not(here))
                    def _():
                        remote(piece, place, ysend.at[part["i"], d - 1, zs, kk], done,
                               device(x, z, yy, kk)).start()

    def y_send_waits(part):
        @pl.loop(1, dists)
        def _(d):
            yy = lax.rem(y - d + 3 * NY, NY)
            for zs in range(2):
                for kk in range(2):
                    here = (yy == y) & (k == kk)
                    piece = part["stage"].at[d - 1, zs, kk]

                    @pl.when(jnp.logical_not(here))
                    def _():
                        remote(piece, piece, ysend.at[part["i"], d - 1, zs, kk],
                               yrecv.at[part["i"], d], device(x, z, yy, kk)).wait_send()

    def z_wait(part, ref, slot):
        pltpu.make_async_copy(ref, ref, zrecv.at[part["i"], slot]).wait()

    def product(part, strips):
        own = jnp.concatenate(
            [part[n][...].reshape(-1, part[n].shape[2]) for n in ("own", "oc0", "p", "ocp")], axis=1
        )
        return lax.dot_general(
            jnp.concatenate(strips, axis=1), own, (((1,), (1,)), ((), ())),
            preferred_element_type=jnp.float32,
        )

    tokens = 4 * b0_a.shape[2]

    def blend(part, d, fresh):
        old = part["old"]
        old[d] = (
            ema_decay * old[d].astype(jnp.float32) + (1.0 - ema_decay) * (fresh / tokens)
        ).astype(jnp.bfloat16)
        pltpu.make_async_copy(old.at[d], part["out"].at[d], out_sem.at[part["i"], d]).start()

    def compute_first():
        for copy in old_copies:
            copy.wait()
        for part in parts:
            for slot in range(2):
                place = part["oc0"] if slot == 0 else part["ocp"]
                pltpu.make_async_copy(place, place, ocrecv.at[part["i"], slot]).wait()
            a = assign_ref[0, q]
            blend(part, 0, product(part, [part[n][a] for n in ("own", "oc0", "p", "ocp")]))

    def compute(lo, hi):
        @pl.loop(lo, hi)
        def _(d):
            for part in parts:
                got = part["recv"].at[d]
                pltpu.make_async_copy(got, got, yrecv.at[part["i"], d]).wait()
                blend(part, d, product(part, [part["recv"][d, r] for r in range(4)]))

    for part in parts:
        if part["i"] == 1:
            shift.wait_recv()
            b0_g[...] = gbuf[...].T.reshape(b0_g.shape)
        z_start(part, "own")
        twin_copy(part, part["own"], part["oc0"], 0).start()
        y_sends(part, part["own"], 0, zl)
    for part in parts:
        z_wait(part, part["p"], 0)
        z_start(part, "p")
        twin_copy(part, part["p"], part["ocp"], 1).start()
        y_sends(part, part["p"], 0, 1 - zl)
    for n in range(4):
        for part in parts:
            block = part["c"][n]
            z_wait(part, block, n + 1)
            z_start(part, "c%d" % n)
            y_sends(part, block, (n + 2) // 2, n % 2)
        if n == 1:
            compute_first()
        if n == 2:
            compute(1, 3)
    compute(3, dists)

    for part in parts:
        for name in ("own", "p", "c0", "c1", "c2", "c3"):
            for condition, copy in flows[part["i"]][name]:
                pl.when(condition)(copy.wait_send)
        twin_copy(part, part["own"], part["oc0"], 0).wait_send()
        twin_copy(part, part["p"], part["ocp"], 1).wait_send()
        y_send_waits(part)
        for d in range(dists):
            pltpu.make_async_copy(part["old"].at[d], part["out"].at[d], out_sem.at[part["i"], d]).wait()
    shift.wait_send()


def on_device(activations, out_grads, assign, act_old, grad_old):
    tokens, act_width = activations.shape[1:]
    grad_width = out_grads.shape[2]
    dists, act_strip = act_old.shape[1:3]
    grad_strip = grad_old.shape[2]
    bf16 = jnp.bfloat16
    vmem = lambda *shape: pltpu.VMEM(shape, bf16)
    dma = pltpu.SemaphoreType.DMA
    any_spec = pl.BlockSpec(memory_space=pl.ANY)
    act_new, grad_new = pl.pallas_call(
        kernel,
        out_shape=(
            jax.ShapeDtypeStruct(act_old.shape[1:], bf16),
            jax.ShapeDtypeStruct(grad_old.shape[1:], bf16),
        ),
        in_specs=[
            pl.BlockSpec(memory_space=pltpu.VMEM),
            any_spec,
            pl.BlockSpec(memory_space=pltpu.SMEM),
            any_spec,
            any_spec,
        ],
        out_specs=(any_spec, any_spec),
        scratch_shapes=[vmem(4, act_strip, tokens)] * 8
        + [vmem(4, grad_strip, tokens)] * 8
        + [
            vmem(tokens, grad_width),
            vmem(dists - 1, 2, 2, act_strip, tokens),
            vmem(dists - 1, 2, 2, grad_strip, tokens),
            vmem(dists, 4, act_strip, tokens),
            vmem(dists, 4, grad_strip, tokens),
            vmem(*act_old.shape[1:]),
            vmem(*grad_old.shape[1:]),
            dma((2,)),
            dma((2, dists)),
            dma((2,)),
            dma((2, 7)),
            dma((2, 5)),
            dma((2, 2)),
            dma((2, 2)),
            dma((2, dists - 1, 2, 2)),
            dma((2, dists)),
        ],
        compiler_params=pltpu.CompilerParams(
            collective_id=0, has_side_effects=True, vmem_limit_bytes=58 * 1024 * 1024
        ),
        cost_estimate=pl.CostEstimate(
            flops=2 * dists * 4 * tokens * (act_strip * act_width + grad_strip * grad_width),
            bytes_accessed=4 * dists * (act_strip * act_width + grad_strip * grad_width),
            transcendentals=0,
        ),
    )(activations[0], out_grads[0], assign, act_old[0], grad_old[0])
    return act_new[None], grad_new[None]


def solution(mesh):
    return jax.shard_map(
        on_device,
        mesh=mesh,
        in_specs=(
            P("section", "dist", "col"),
            P("section", "dist", "col"),
            P(),
            P("section", None, "dist", "col"),
            P("section", None, "dist", "col"),
        ),
        out_specs=(P("section", None, "dist", "col"), P("section", None, "dist", "col")),
        check_vma=False,
    )
```

```python
import jax
import jax.numpy as jnp
from jax import lax
from jax.experimental import pallas as pl
from jax.experimental.pallas import tpu as pltpu
from jax.sharding import PartitionSpec as P

ema_decay = 0.75
MESH = pl.DeviceIdType.MESH
NY = 4
NZ = 8
NX = 4


NAMES = ("own", "p", "c0", "c1", "c2", "c3", "oc0", "ocp")
ACT_PARTS, GRAD_PARTS = 4, 2
HALVES = 2
SAME = ("own", "oc0", "p", "ocp")


STEPS = (
    (
        (("own",), ("p",), ("c0", "c3"), ("c2", "c1"), ()),
        (("own",), ("p",), ("c0",), ("c1",), ("c3", "c2")),
    ),
    ((("own",), ("c0", "p"), ("c1",), ("c2",), ("c3",)),) * 2,
)
FIRST = (0,0,1,2,3,3)


def arrivals(parity):
    for step in range(len(STEPS[0][0]) + max(FIRST)):
        for i, first in enumerate(FIRST):
            steps = STEPS[parity][0 if i < ACT_PARTS else 1]
            if 0 <= step - first < len(steps):
                for name in steps[step - first]:
                    yield i, name


def kernel(act_ref, og_ref, assign_hbm, olda_hbm, oldg_hbm, olda, oldg, *scratch):
    scratch = list(scratch)
    parts = []
    for i in range(ACT_PARTS + GRAD_PARTS):
        part = {name: scratch.pop(0) for name in NAMES}
        part.update(i=i, act=i < ACT_PARTS, stage=scratch.pop(0))
        parts.append(part)
    (recv_a, recv_g, gbuf, assign_ref, assign_sem,
     old_sem, shift_sem, zsend, zrecv, ocsend, ocrecv, ysend, yrecv) = scratch
    x = lax.axis_index("section")
    c = lax.axis_index("col")
    q = lax.axis_index("dist")
    y, zh = lax.rem(c, NY), c // NY
    zl, k = q // 2, lax.rem(q, 2)
    z = 2 * zh + zl
    dists = olda.shape[0]
    for part in parts:
        kind = 0 if part["act"] else 1
        part.update(kind=kind, recv=(recv_a, recv_g)[kind], n=part["i"] - kind * ACT_PARTS)
    acts, grads = parts[:ACT_PARTS], parts[ACT_PARTS:]
    kinds = tuple(
        dict(i=i, old=old, recv=(recv_a, recv_g)[i], halves=[own[h::HALVES] for h in range(HALVES)])
        for i, own, old in ((0, acts, olda), (1, grads, oldg))
    )

    def device(xx, zz, yy, kk):
        return (xx, (zz // 2) * NY + yy, lax.rem(zz, 2) * 2 + kk)

    z_down = device(x, lax.rem(z + NZ - 1, NZ), y, k)
    z_up = device(x, lax.rem(z + 1, NZ), y, k)
    z_far = device(x, lax.rem(z + 3, NZ), y, k)
    z_back = device(x, lax.rem(z + NZ - 3, NZ), y, k)
    twin = device(x, z, y, 1 - k)
    x_down = device(lax.rem(x + NX - 1, NX), z, y, k)
    x_up = device(lax.rem(x + 1, NX), z, y, k)

    old_copies = [
        pltpu.make_async_copy(olda_hbm, olda, old_sem.at[0]),
        pltpu.make_async_copy(oldg_hbm, oldg, old_sem.at[1]),
    ]
    assign_copy = pltpu.make_async_copy(assign_hbm, assign_ref, assign_sem)

    barrier = pltpu.get_barrier_semaphore()
    greeted = [z_down, z_up, z_far, z_back, twin, x_down, x_up]
    for step in range(1, NY):
        for kk in range(2):
            greeted.append(device(x, z, lax.rem(y + step, NY), kk))
    for other in greeted:
        pl.semaphore_signal(barrier, inc=1, device_id=other, device_id_type=MESH)
    assign_copy.start()
    for copy in old_copies:
        copy.start()
    lanes = act_ref.shape[0] // HALVES

    def place_own(kind, rows_ref):
        for h, members in enumerate(kind["halves"]):
            turned = rows_ref[pl.ds(h * lanes, lanes), :].T.reshape(4, -1, lanes)
            height = turned.shape[1] // len(members)
            for r, part in enumerate(members):
                part["own"][...] = turned[:, r * height:(r + 1) * height]

    place_own(kinds[0], act_ref)
    assign_copy.wait()
    pl.semaphore_wait(barrier, len(greeted))

    def remote(src, dst, send, recv, target):
        return pltpu.make_async_remote_copy(
            src_ref=src, dst_ref=dst, send_sem=send, recv_sem=recv,
            device_id=target, device_id_type=MESH,
        )

    shift = remote(og_ref, gbuf, shift_sem.at[0], shift_sem.at[1], x_down)
    shift.start()

    def z_copy(part, src, slot, dst, dst_slot, target):
        return remote(src, dst, zsend.at[part["i"], slot], zrecv.at[part["i"], dst_slot], target)

    def twin_copy(part, src, dst, slot):
        return remote(src, dst, ocsend.at[part["i"], slot], ocrecv.at[part["i"], slot], twin)

    def z_flows(part):
        cs = tuple(part["c%d" % n] for n in range(4))
        flows = {
            "own": [
                (1, z_copy(part, part["own"], 0, part["p"], 0, z_down)),
                (0, z_copy(part, part["own"], 0, cs[0], 1, z_down)),
                (0, z_copy(part, part["own"], 6, part["p"], 0, z_up)),
                (1, z_copy(part, part["own"], 6, cs[3], 4, z_far)),
            ],
            "p": [(0, z_copy(part, part["p"], 1, cs[1], 2, z_down))],
            "c0": [
                (0, z_copy(part, cs[0], 2, cs[2], 3, z_down)),
                (1, z_copy(part, cs[0], 2, cs[0], 1, z_down)),
            ],
            "c1": [(1, z_copy(part, cs[1], 3, cs[1], 2, z_down))],
            "c2": [],
            "c3": [],
        }
        if part["act"]:
            flows["p"].append((1, z_copy(part, part["p"], 7, cs[2], 3, z_far)))
            flows["c3"].append((0, z_copy(part, cs[3], 7, cs[3], 4, z_up)))
        else:
            flows["c1"].append((0, z_copy(part, cs[1], 3, cs[3], 4, z_down)))
            flows["c2"].append((1, z_copy(part, cs[2], 4, cs[2], 3, z_down)))
        return flows

    flows = [z_flows(part) for part in parts]

    def z_start(part, name, parity):
        for wanted, copy in flows[part["i"]][name]:
            if wanted == parity:
                copy.start()

    columns = [zh * NY + jnp.where(y + r >= NY, y + r - NY, y + r) for r in range(NY)]

    def y_sends(part, source, parity, dzh, zs):
        for r in range(NY):
            if dzh == 0 and r == 0:
                continue
            d = c + NY * dzh - columns[r]

            def send():
                for other in range(2):
                    kk = 1 - k if other else k
                    piece = part["stage"].at[d - 1, zs, other]
                    piece[...] = source[assign_ref[2 * parity + kk, d]]
                    place = part["recv"].at[d, part["n"], 2 * (zs != parity) + other]
                    done = yrecv.at[part["kind"], d]
                    if r == 0 and other == 0:
                        pltpu.make_async_copy(piece, place, done).start()
                    else:
                        remote(piece, place, ysend.at[part["i"]], done,
                               (x, columns[r], 2 * parity + kk)).start()

            if dzh == 1 or r == 0:
                send()
            else:
                pl.when(d >= 1 if dzh == 0 else d < dists)(send)

    def y_send_wait(part):
        sent = part["stage"].at[pl.ds(0, dists - 2)]
        pltpu.make_async_copy(sent, sent, ysend.at[part["i"]]).wait()

    def z_wait(part, ref, slot):
        pltpu.make_async_copy(ref, ref, zrecv.at[part["i"], slot]).wait()

    def product(kind, strips_of):
        own = jnp.concatenate([
            jnp.concatenate([p[n][a] for a in range(4) for p in members], axis=0)
            for members in kind["halves"] for n in SAME
        ], axis=1)
        strips = jnp.concatenate([
            jnp.concatenate(strips_of(members, slot), axis=0)
            for members in kind["halves"] for slot in range(len(SAME))
        ], axis=1)
        return lax.dot_general(
            strips, own, (((1,), (1,)), ((), ())), preferred_element_type=jnp.float32
        )

    tokens = 4 * act_ref.shape[0]

    def blend(kind, d, fresh):
        old = kind["old"]
        old[d] = (
            ema_decay * old[d].astype(jnp.float32) + (1.0 - ema_decay) * (fresh / tokens)
        ).astype(jnp.bfloat16)

    def compute_first(kind):
        old_copies[kind["i"]].wait()
        for part in sum(kind["halves"], []):
            for slot in range(2):
                place = part["oc0"] if slot == 0 else part["ocp"]
                pltpu.make_async_copy(place, place, ocrecv.at[part["i"], slot]).wait()
        a = assign_ref[q, 0]
        blend(kind, 0, product(kind, lambda members, slot: [p[SAME[slot]][a] for p in members]))

    count = 2

    def compute(kind, lo, hi):
        @pl.loop(lo, hi)
        def _(group):
            members = [group * count + 1 + n for n in range(count)]
            for d in members:
                got = kind["recv"].at[d]
                pltpu.make_async_copy(got, got, yrecv.at[kind["i"], d]).wait()
            fresh = product(
                kind, lambda those, slot: [p["recv"][d, p["n"], slot] for d in members for p in those]
            )
            height = fresh.shape[0] // count
            for n, d in enumerate(members):
                blend(kind, d, fresh[n * height:(n + 1) * height])

    def arrived(i, name, parity):
        part = parts[i]
        if name == "own":
            if i == ACT_PARTS:
                shift.wait_recv()
                place_own(kinds[1], gbuf)
            z_start(part, "own", parity)
            twin_copy(part, part["own"], part["oc0"], 0).start()
            y_sends(part, part["own"], parity, 0, parity)
        elif name == "p":
            z_wait(part, part["p"], 0)
            z_start(part, "p", parity)
            twin_copy(part, part["p"], part["ocp"], 1).start()
            y_sends(part, part["p"], parity, 0, 1 - parity)
        else:
            n = int(name[1])
            z_wait(part, part[name], n + 1)
            z_start(part, name, parity)
            y_sends(part, part[name], parity, (n + 2) // 2, n % 2)

    for parity in range(2):

        @pl.when(zl == parity)
        def _():
            for i, name in arrivals(parity):
                arrived(i, name, parity)

    groups = (dists - 1) // count
    compute_first(kinds[0])
    compute(kinds[0], 0, groups)
    compute_first(kinds[1])
    for parity in range(2):

        @pl.when(zl == parity)
        def _():
            for part in parts:
                for name in NAMES[:6]:
                    for wanted, copy in flows[part["i"]][name]:
                        if wanted == parity:
                            copy.wait_send()

    for part in parts:
        twin_copy(part, part["own"], part["oc0"], 0).wait_send()
        twin_copy(part, part["p"], part["ocp"], 1).wait_send()
    compute(kinds[1], 0, groups)
    for part in parts:
        y_send_wait(part)
    shift.wait_send()


def on_device(activations, out_grads, assign, act_old, grad_old):
    tokens, act_width = activations.shape[1:]
    grad_width = out_grads.shape[2]
    dists, act_strip = act_old.shape[1:3]
    grad_strip = grad_old.shape[2]
    bf16 = jnp.bfloat16
    vmem = lambda *shape: pltpu.VMEM(shape, bf16)
    dma = pltpu.SemaphoreType.DMA
    half = tokens // HALVES
    count = ACT_PARTS + GRAD_PARTS
    any_spec = pl.BlockSpec(memory_space=pl.ANY)
    vmem_spec = pl.BlockSpec(memory_space=pltpu.VMEM)
    act_new, grad_new = pl.pallas_call(
        kernel,
        out_shape=(
            vmem(*act_old.shape[1:]),
            vmem(*grad_old.shape[1:]),
        ),
        in_specs=[
            vmem_spec,
            any_spec,
            any_spec,
            any_spec,
            any_spec,
        ],
        out_specs=(vmem_spec, vmem_spec),
        scratch_shapes=[
            vmem(*shape)
            for rows, lanes in ((act_strip * HALVES // ACT_PARTS, half),) * ACT_PARTS
            + ((grad_strip * HALVES // GRAD_PARTS, half),) * GRAD_PARTS
            for shape in [(4, rows, lanes)] * len(NAMES)
            + [(dists - 1, 2, 2, rows, lanes)]
        ]
        + [
            vmem(dists, ACT_PARTS, 4, act_strip * HALVES // ACT_PARTS, half),
            vmem(dists, GRAD_PARTS, 4, grad_strip * HALVES // GRAD_PARTS, half),
            vmem(tokens, grad_width),
            pltpu.SMEM(assign.shape[::-1], jnp.int32),
            dma,
            dma((2,)),
            dma((2,)),
            dma((count, 8)),
            dma((count, 5)),
            dma((count, 2)),
            dma((count, 2)),
            dma((count,)),
            dma((2, dists)),
        ],
        compiler_params=pltpu.CompilerParams(
            collective_id=0, has_side_effects=True, vmem_limit_bytes=57 * 1024 * 1024
        ),
        cost_estimate=pl.CostEstimate(
            flops=2 * dists * 4 * tokens * (act_strip * act_width + grad_strip * grad_width),
            bytes_accessed=4 * dists * (act_strip * act_width + grad_strip * grad_width),
            transcendentals=0,
        ),
    )(activations[0], out_grads[0], assign.T, act_old[0], grad_old[0])
    return act_new[None], grad_new[None]


def solution(mesh):
    return jax.shard_map(
        on_device,
        mesh=mesh,
        in_specs=(
            P("section", "dist", "col"),
            P("section", "dist", "col"),
            P(),
            P("section", None, "dist", "col"),
            P("section", None, "dist", "col"),
        ),
        out_specs=(P("section", None, "dist", "col"), P("section", None, "dist", "col")),
        check_vma=False,
    )
```

```python
import jax
import jax.numpy as jnp
from jax import lax
from jax.experimental import pallas as pl
from jax.experimental.pallas import tpu as pltpu
from jax.sharding import PartitionSpec as P

ema_decay = 0.75
MESH = pl.DeviceIdType.MESH
NY = 4
NZ = 8
NX = 4


NAMES = ("own", "p", "c0", "c1", "c2", "c3", "oc0", "ocp")
ACT_PARTS, GRAD_PARTS = 4, 2
HALVES = 2
SAME = ("own", "oc0", "p", "ocp")


STEPS = (
    (
        (("own",), ("p",), ("c0", "c3"), ("c2", "c1"), ()),
        (("own",), ("p",), ("c0",), ("c1",), ("c3", "c2")),
    ),
    ((("own",), ("c0", "p"), ("c1",), ("c2",), ("c3",)),) * 2,
)
FIRST = (0,0,1,2,3,3)


def arrivals(parity):
    for step in range(len(STEPS[0][0]) + max(FIRST)):
        for i, first in enumerate(FIRST):
            steps = STEPS[parity][0 if i < ACT_PARTS else 1]
            if 0 <= step - first < len(steps):
                for name in steps[step - first]:
                    yield i, name


def kernel(act_ref, og_ref, assign_hbm, olda_hbm, oldg_hbm, olda, oldg, *scratch):
    scratch = list(scratch)
    parts = []
    for i in range(ACT_PARTS + GRAD_PARTS):
        part = {name: scratch.pop(0) for name in NAMES}
        part.update(i=i, act=i < ACT_PARTS, stage=scratch.pop(0))
        parts.append(part)
    (recv_a, recv_g, gbuf, assign_ref, assign_sem,
     old_sem, shift_sem, zsend, zrecv, ocsend, ocrecv, ysend, yrecv) = scratch
    x = lax.axis_index("section")
    c = lax.axis_index("col")
    q = lax.axis_index("dist")
    y, zh = lax.rem(c, NY), c // NY
    zl, k = q // 2, lax.rem(q, 2)
    z = 2 * zh + zl
    dists = olda.shape[0]
    for part in parts:
        kind = 0 if part["act"] else 1
        part.update(kind=kind, recv=(recv_a, recv_g)[kind], n=part["i"] - kind * ACT_PARTS)
    acts, grads = parts[:ACT_PARTS], parts[ACT_PARTS:]
    kinds = tuple(
        dict(i=i, old=old, recv=(recv_a, recv_g)[i], halves=[own[h::HALVES] for h in range(HALVES)])
        for i, own, old in ((0, acts, olda), (1, grads, oldg))
    )

    def device(xx, zz, yy, kk):
        return (xx, (zz // 2) * NY + yy, lax.rem(zz, 2) * 2 + kk)

    z_down = device(x, lax.rem(z + NZ - 1, NZ), y, k)
    z_up = device(x, lax.rem(z + 1, NZ), y, k)
    z_far = device(x, lax.rem(z + 3, NZ), y, k)
    z_back = device(x, lax.rem(z + NZ - 3, NZ), y, k)
    twin = device(x, z, y, 1 - k)
    x_down = device(lax.rem(x + NX - 1, NX), z, y, k)
    x_up = device(lax.rem(x + 1, NX), z, y, k)

    old_copies = [
        pltpu.make_async_copy(olda_hbm, olda, old_sem.at[0]),
        pltpu.make_async_copy(oldg_hbm, oldg, old_sem.at[1]),
    ]
    assign_copy = pltpu.make_async_copy(assign_hbm, assign_ref, assign_sem)

    barrier = pltpu.get_barrier_semaphore()
    greeted = [z_down, z_up, z_far, z_back, twin, x_down, x_up]
    for step in range(1, NY):
        for kk in range(2):
            greeted.append(device(x, z, lax.rem(y + step, NY), kk))
    for other in greeted:
        pl.semaphore_signal(barrier, inc=1, device_id=other, device_id_type=MESH)
    assign_copy.start()
    for copy in old_copies:
        copy.start()
    lanes = act_ref.shape[0] // HALVES

    def place_own(kind, rows_ref):
        for h, members in enumerate(kind["halves"]):
            turned = rows_ref[pl.ds(h * lanes, lanes), :].T.reshape(4, -1, lanes)
            height = turned.shape[1] // len(members)
            for r, part in enumerate(members):
                part["own"][...] = turned[:, r * height:(r + 1) * height]

    place_own(kinds[0], act_ref)
    assign_copy.wait()
    pl.semaphore_wait(barrier, len(greeted))

    def remote(src, dst, send, recv, target):
        return pltpu.make_async_remote_copy(
            src_ref=src, dst_ref=dst, send_sem=send, recv_sem=recv,
            device_id=target, device_id_type=MESH,
        )

    shift = remote(og_ref, gbuf, shift_sem.at[0], shift_sem.at[1], x_down)
    shift.start()

    def z_copy(part, src, slot, dst, dst_slot, target):
        return remote(src, dst, zsend.at[part["i"], slot], zrecv.at[part["i"], dst_slot], target)

    def twin_copy(part, src, dst, slot):
        return remote(src, dst, ocsend.at[part["i"], slot], ocrecv.at[part["i"], slot], twin)

    def z_flows(part):
        cs = tuple(part["c%d" % n] for n in range(4))
        flows = {
            "own": [
                (1, z_copy(part, part["own"], 0, part["p"], 0, z_down)),
                (0, z_copy(part, part["own"], 0, cs[0], 1, z_down)),
                (0, z_copy(part, part["own"], 6, part["p"], 0, z_up)),
                (1, z_copy(part, part["own"], 6, cs[3], 4, z_far)),
            ],
            "p": [(0, z_copy(part, part["p"], 1, cs[1], 2, z_down))],
            "c0": [
                (0, z_copy(part, cs[0], 2, cs[2], 3, z_down)),
                (1, z_copy(part, cs[0], 2, cs[0], 1, z_down)),
            ],
            "c1": [(1, z_copy(part, cs[1], 3, cs[1], 2, z_down))],
            "c2": [],
            "c3": [],
        }
        if part["act"]:
            flows["p"].append((1, z_copy(part, part["p"], 7, cs[2], 3, z_far)))
            flows["c3"].append((0, z_copy(part, cs[3], 7, cs[3], 4, z_up)))
        else:
            flows["c1"].append((0, z_copy(part, cs[1], 3, cs[3], 4, z_down)))
            flows["c2"].append((1, z_copy(part, cs[2], 4, cs[2], 3, z_down)))
        return flows

    flows = [z_flows(part) for part in parts]

    def z_start(part, name, parity):
        for wanted, copy in flows[part["i"]][name]:
            if wanted == parity:
                copy.start()

    columns = [zh * NY + jnp.where(y + r >= NY, y + r - NY, y + r) for r in range(NY)]

    def y_sends(part, source, parity, dzh, zs):
        for r in (2, 1, 3, 0):
            if dzh == 0 and r == 0:
                continue
            d = c + NY * dzh - columns[r]

            def send():
                for other in range(2):
                    kk = 1 - k if other else k
                    piece = part["stage"].at[d - 1, zs, other]
                    piece[...] = source[assign_ref[2 * parity + kk, d]]
                    place = part["recv"].at[d, part["n"], 2 * (zs != parity) + other]
                    done = yrecv.at[part["kind"], d]
                    if r == 0 and other == 0:
                        pltpu.make_async_copy(piece, place, done).start()
                    else:
                        remote(piece, place, ysend.at[part["i"]], done,
                               (x, columns[r], 2 * parity + kk)).start()

            if dzh == 1 or r == 0:
                send()
            else:
                pl.when(d >= 1 if dzh == 0 else d < dists)(send)

    def y_send_wait(part):
        sent = part["stage"].at[pl.ds(0, dists - 2)]
        pltpu.make_async_copy(sent, sent, ysend.at[part["i"]]).wait()

    def z_wait(part, ref, slot):
        pltpu.make_async_copy(ref, ref, zrecv.at[part["i"], slot]).wait()

    def product(kind, strips_of):
        own = jnp.concatenate([
            jnp.concatenate([p[n][a] for a in range(4) for p in members], axis=0)
            for members in kind["halves"] for n in SAME
        ], axis=1)
        strips = jnp.concatenate([
            jnp.concatenate(strips_of(members, slot), axis=0)
            for members in kind["halves"] for slot in range(len(SAME))
        ], axis=1)
        return lax.dot_general(
            strips, own, (((1,), (1,)), ((), ())), preferred_element_type=jnp.float32
        )

    tokens = 4 * act_ref.shape[0]

    def blend(kind, d, fresh):
        old = kind["old"]
        old[d] = (
            ema_decay * old[d].astype(jnp.float32) + (1.0 - ema_decay) * (fresh / tokens)
        ).astype(jnp.bfloat16)

    def compute_first(kind):
        old_copies[kind["i"]].wait()
        for part in sum(kind["halves"], []):
            for slot in range(2):
                place = part["oc0"] if slot == 0 else part["ocp"]
                pltpu.make_async_copy(place, place, ocrecv.at[part["i"], slot]).wait()
        a = assign_ref[q, 0]
        blend(kind, 0, product(kind, lambda members, slot: [p[SAME[slot]][a] for p in members]))

    count = 2

    def compute(kind, lo, hi):
        @pl.loop(lo, hi)
        def _(group):
            members = [group * count + 1 + n for n in range(count)]
            for d in members:
                got = kind["recv"].at[d]
                pltpu.make_async_copy(got, got, yrecv.at[kind["i"], d]).wait()
            fresh = product(
                kind, lambda those, slot: [p["recv"][d, p["n"], slot] for d in members for p in those]
            )
            height = fresh.shape[0] // count
            for n, d in enumerate(members):
                blend(kind, d, fresh[n * height:(n + 1) * height])

    def arrived(i, name, parity):
        part = parts[i]
        if name == "own":
            if i == ACT_PARTS:
                shift.wait_recv()
                place_own(kinds[1], gbuf)
            z_start(part, "own", parity)
            twin_copy(part, part["own"], part["oc0"], 0).start()
            y_sends(part, part["own"], parity, 0, parity)
        elif name == "p":
            z_wait(part, part["p"], 0)
            z_start(part, "p", parity)
            twin_copy(part, part["p"], part["ocp"], 1).start()
            y_sends(part, part["p"], parity, 0, 1 - parity)
        else:
            n = int(name[1])
            z_wait(part, part[name], n + 1)
            z_start(part, name, parity)
            y_sends(part, part[name], parity, (n + 2) // 2, n % 2)

    for parity in range(2):

        @pl.when(zl == parity)
        def _():
            for i, name in arrivals(parity):
                if (i, name) == (len(parts) - 1, "c2" if parity == 0 else "c3"):
                    for kind in kinds:
                        compute_first(kind)
                arrived(i, name, parity)

    groups = (dists - 1) // count
    compute(kinds[0], 0, groups)
    for parity in range(2):

        @pl.when(zl == parity)
        def _():
            for part in parts:
                for name in NAMES[:6]:
                    for wanted, copy in flows[part["i"]][name]:
                        if wanted == parity:
                            copy.wait_send()

    for part in parts:
        twin_copy(part, part["own"], part["oc0"], 0).wait_send()
        twin_copy(part, part["p"], part["ocp"], 1).wait_send()
    compute(kinds[1], 0, groups)
    for part in parts:
        y_send_wait(part)
    shift.wait_send()


def on_device(activations, out_grads, assign, act_old, grad_old):
    tokens, act_width = activations.shape[1:]
    grad_width = out_grads.shape[2]
    dists, act_strip = act_old.shape[1:3]
    grad_strip = grad_old.shape[2]
    bf16 = jnp.bfloat16
    vmem = lambda *shape: pltpu.VMEM(shape, bf16)
    dma = pltpu.SemaphoreType.DMA
    half = tokens // HALVES
    count = ACT_PARTS + GRAD_PARTS
    any_spec = pl.BlockSpec(memory_space=pl.ANY)
    vmem_spec = pl.BlockSpec(memory_space=pltpu.VMEM)
    act_new, grad_new = pl.pallas_call(
        kernel,
        out_shape=(
            vmem(*act_old.shape[1:]),
            vmem(*grad_old.shape[1:]),
        ),
        in_specs=[
            vmem_spec,
            any_spec,
            any_spec,
            any_spec,
            any_spec,
        ],
        out_specs=(vmem_spec, vmem_spec),
        scratch_shapes=[
            vmem(*shape)
            for rows, lanes in ((act_strip * HALVES // ACT_PARTS, half),) * ACT_PARTS
            + ((grad_strip * HALVES // GRAD_PARTS, half),) * GRAD_PARTS
            for shape in [(4, rows, lanes)] * len(NAMES)
            + [(dists - 1, 2, 2, rows, lanes)]
        ]
        + [
            vmem(dists, ACT_PARTS, 4, act_strip * HALVES // ACT_PARTS, half),
            vmem(dists, GRAD_PARTS, 4, grad_strip * HALVES // GRAD_PARTS, half),
            vmem(tokens, grad_width),
            pltpu.SMEM(assign.shape[::-1], jnp.int32),
            dma,
            dma((2,)),
            dma((2,)),
            dma((count, 8)),
            dma((count, 5)),
            dma((count, 2)),
            dma((count, 2)),
            dma((count,)),
            dma((2, dists)),
        ],
        compiler_params=pltpu.CompilerParams(
            collective_id=0, has_side_effects=True, vmem_limit_bytes=57 * 1024 * 1024
        ),
        cost_estimate=pl.CostEstimate(
            flops=2 * dists * 4 * tokens * (act_strip * act_width + grad_strip * grad_width),
            bytes_accessed=4 * dists * (act_strip * act_width + grad_strip * grad_width),
            transcendentals=0,
        ),
    )(activations[0], out_grads[0], assign.T, act_old[0], grad_old[0])
    return act_new[None], grad_new[None]


def solution(mesh):
    return jax.shard_map(
        on_device,
        mesh=mesh,
        in_specs=(
            P("section", "dist", "col"),
            P("section", "dist", "col"),
            P(),
            P("section", None, "dist", "col"),
            P("section", None, "dist", "col"),
        ),
        out_specs=(P("section", None, "dist", "col"), P("section", None, "dist", "col")),
        check_vma=False,
    )
```
